32 devices in a mesh: dp: 8 (over y, x, core), tp: 4 (over z).
Axes of the slice: x: 2, y: 2, z: 4, core: 2. Of those that a mesh axis runs over, the one named last changes fastest.
Arguments:
- rows_in: bfloat16 [8192, 1024], P(('dp', 'tp')), may hold values from -6 to 6
- memory: bfloat16 [4096, 1024], P(('dp', 'tp')), may hold values from -6 to 6
- lengths: int32 [8], P('dp'), may hold values from 256 to 1024, as said below
- mem_lengths: int32 [8], P('dp'), may hold values from 128 to 512, as said below
- cotangent: bfloat16 [8192, 1024], P(('dp', 'tp')), may hold values from -6 to 6
- query_w: float32 [1024, 1024], P('dp', 'tp'), may hold values from -0.1875 to 0.1875
- keyval_w: float32 [2, 1024, 512], P(None, 'dp', 'tp'), may hold values from -0.1875 to 0.1875
- out_w: float32 [1024, 1024], P('tp', 'dp'), may hold values from -2 to 2
- cross_query_w: float32 [1024, 1024], P('dp', 'tp'), may hold values from -0.1875 to 0.1875
- cross_keyval_w: float32 [2, 1024, 512], P(None, 'dp', 'tp'), may hold values from -0.1875 to 0.1875
- cross_out_w: float32 [1024, 1024], P('tp', 'dp'), may hold values from -1.5 to 1.5
- gateup_w: float32 [2, 1024, 2816], P(None, 'dp', 'tp'), may hold values from -0.1875 to 0.1875
- down_w: float32 [2816, 1024], P('tp', 'dp'), may hold values from -0.109375 to 0.109375
- gains: float32 [3, 1024], P(None, 'dp'), may hold values from 0.5 to 1.5
- rel_table: float32 [16, 32], P('tp', 'dp'), may hold values from -4 to 4
- query_m: float32 [1024, 1024], P('dp', 'tp'), may hold values from -0.0004272461 to 0.0004272461
- keyval_m: float32 [2, 1024, 512], P(None, 'dp', 'tp'), may hold values from -0.0004272461 to 0.0004272461
- out_m: float32 [1024, 1024], P('tp', 'dp'), may hold values from -0.00010681152 to 0.00010681152
- cross_query_m: float32 [1024, 1024], P('dp', 'tp'), may hold values from -0.0004272461 to 0.0004272461
- cross_keyval_m: float32 [2, 1024, 512], P(None, 'dp', 'tp'), may hold values from -0.0004272461 to 0.0004272461
- cross_out_m: float32 [1024, 1024], P('tp', 'dp'), may hold values from -7.6293945e-05 to 7.6293945e-05
- gateup_m: float32 [2, 1024, 2816], P(None, 'dp', 'tp'), may hold values from -0.00018310547 to 0.00018310547
- down_m: float32 [2816, 1024], P('tp', 'dp'), may hold values from -0.0004272461 to 0.0004272461
- gains_m: float32 [3, 1024], P(None, 'dp'), may hold values from -0.0017089844 to 0.0017089844
- rel_table_m: float32 [16, 32], P('tp', 'dp'), may hold values from -0.0017089844 to 0.0017089844
- query_v: float32 [1024, 1024], P('dp', 'tp'), may hold values from 3.5461487e-09 to 1.4050777e-08
- keyval_v: float32 [2, 1024, 512], P(None, 'dp', 'tp'), may hold values from 3.5461487e-09 to 1.4050777e-08
- out_v: float32 [1024, 1024], P('tp', 'dp'), may hold values from 2.141071e-10 to 8.4304663e-10
- cross_query_v: float32 [1024, 1024], P('dp', 'tp'), may hold values from 3.5461487e-09 to 1.4050777e-08
- cross_keyval_v: float32 [2, 1024, 512], P(None, 'dp', 'tp'), may hold values from 3.5461487e-09 to 1.4050777e-08
- cross_out_v: float32 [1024, 1024], P('tp', 'dp'), may hold values from 1.4050777e-10 to 5.620311e-10
- gateup_v: float32 [2, 1024, 2816], P(None, 'dp', 'tp'), may hold values from 7.0922973e-10 to 2.8101554e-09
- down_v: float32 [2816, 1024], P('tp', 'dp'), may hold values from 3.5461487e-09 to 1.4050777e-08
- gains_v: float32 [3, 1024], P(None, 'dp'), may hold values from 5.620311e-08 to 2.2748878e-07
- rel_table_v: float32 [16, 32], P('tp', 'dp'), may hold values from 5.620311e-08 to 2.2748878e-07
Outputs:
- block_out: bfloat16 [8192, 1024], P(('dp', 'tp'))
- grad_rows: float32 [8192, 1024], P(('dp', 'tp'))
- grad_memory: float32 [4096, 1024], P(('dp', 'tp'))
- grad_norm: float32 [], replicated
- new_query_m: float32 [1024, 1024], P('dp', 'tp')
- new_keyval_m: float32 [2, 1024, 512], P(None, 'dp', 'tp')
- new_out_m: float32 [1024, 1024], P('tp', 'dp')
- new_cross_query_m: float32 [1024, 1024], P('dp', 'tp')
- new_cross_keyval_m: float32 [2, 1024, 512], P(None, 'dp', 'tp')
- new_cross_out_m: float32 [1024, 1024], P('tp', 'dp')
- new_gateup_m: float32 [2, 1024, 2816], P(None, 'dp', 'tp')
- new_down_m: float32 [2816, 1024], P('tp', 'dp')
- new_gains_m: float32 [3, 1024], P(None, 'dp')
- new_rel_table_m: float32 [16, 32], P('tp', 'dp')
- new_query_v: float32 [1024, 1024], P('dp', 'tp')
- new_keyval_v: float32 [2, 1024, 512], P(None, 'dp', 'tp')
- new_out_v: float32 [1024, 1024], P('tp', 'dp')
- new_cross_query_v: float32 [1024, 1024], P('dp', 'tp')
- new_cross_keyval_v: float32 [2, 1024, 512], P(None, 'dp', 'tp')
- new_cross_out_v: float32 [1024, 1024], P('tp', 'dp')
- new_gateup_v: float32 [2, 1024, 2816], P(None, 'dp', 'tp')
- new_down_v: float32 [2816, 1024], P('tp', 'dp')
- new_gains_v: float32 [3, 1024], P(None, 'dp')
- new_rel_table_v: float32 [16, 32], P('tp', 'dp')
- new_query_w: float32 [1024, 1024], P('dp', 'tp')
- new_keyval_w: float32 [2, 1024, 512], P(None, 'dp', 'tp')
- new_out_w: float32 [1024, 1024], P('tp', 'dp')
- new_cross_query_w: float32 [1024, 1024], P('dp', 'tp')
- new_cross_keyval_w: float32 [2, 1024, 512], P(None, 'dp', 'tp')
- new_cross_out_w: float32 [1024, 1024], P('tp', 'dp')
- new_gateup_w: float32 [2, 1024, 2816], P(None, 'dp', 'tp')
- new_down_w: float32 [2816, 1024], P('tp', 'dp')
- new_gains: float32 [3, 1024], P(None, 'dp')
- new_rel_table: float32 [16, 32], P('tp', 'dp')
The draws below stay inside these ranges and needn't reach their ends.
Inputs may be any that keep to these rules, and one draw needn't show every extreme that they name: `lengths`: exactly one of the 8 sequences has length 1024. `mem_lengths`: exactly one of the 8 sequences has 512 valid memory rows.
All inputs are finite; a program needn't handle non-finite values.
Results may differ from the reference program's by a relative error of at most 0.023.
Values may be sent and summed in bfloat16 or wider, within the bound.
A program may use at most 192 MiB of HBM per device.

```python
import math
import jax
import jax.numpy as jnp
import numpy as np
from jax import lax

D = 1024
H = 16
KV = 8
DH = 64
FF = 2816
BUCKETS = 32
SEQ_LEN = 1024
MEM = 512
STEP = 10
NSEQ = 8
TOKENS = 8192
MEM_ALL = 4096
NPARAMS = 14945792


def draw_lengths(key, part):
    key = jax.random.fold_in(key, 11)
    first_key, second_key = jax.random.split(key)
    drawn = jax.random.randint(first_key, (NSEQ,), SEQ_LEN // 4, SEQ_LEN)
    chosen = jax.random.randint(second_key, (), 0, NSEQ)
    full_mask = jnp.arange(NSEQ) == chosen
    return jnp.where(full_mask, SEQ_LEN, drawn).astype(jnp.int32)


def draw_mem_lengths(key, part):
    key = jax.random.fold_in(key, 13)
    first_key, second_key = jax.random.split(key)
    drawn = jax.random.randint(first_key, (NSEQ,), MEM // 4, MEM)
    chosen = jax.random.randint(second_key, (), 0, NSEQ)
    full_mask = jnp.arange(NSEQ) == chosen
    return jnp.where(full_mask, MEM, drawn).astype(jnp.int32)


def level_of(key, shape, cuts, low, largest):
    level = 1.0
    for dim, blocks in cuts:
        steps = jax.random.uniform(jax.random.fold_in(jax.random.fold_in(key, 6), dim), (blocks,), jnp.float32, low / len(cuts), largest / len(cuts))
        level = level * jnp.repeat(jnp.exp(steps), shape[dim] // blocks).reshape((-1,) + (1,) * (len(shape) - 1 - dim))
    return level


def noise(own_key, dims, deviation, bound, pieces=(), kind=jnp.bfloat16):
    result = jax.random.normal(own_key, dims, jnp.float32) * deviation
    if len(pieces) > 0:
        result = level_of(own_key, dims, pieces, -0.22, 0.18) * result
    return jnp.clip(result, min=-bound, max=bound).astype(kind)


def setup_inputs(seed: int = 0) -> dict:
    keys = jax.random.split(jax.random.key(seed), 36)
    rows_in = noise(keys[0], (TOKENS, D), 1.0, 6.0, ((0, 32),))
    memory = noise(keys[1], (MEM_ALL, D), 1.0, 6.0, ((0, 32),))
    lengths = draw_lengths(jax.random.fold_in(keys[35], 71), 0)
    mem_lengths = draw_mem_lengths(jax.random.fold_in(keys[35], 71), 0)
    cotangent = noise(keys[4], (TOKENS, D), 1.0, 6.0, ((0, 32),))
    query_w = noise(keys[5], (D, H * DH), D ** -0.5, 0.1875, ((0, 8), (1, 4)), jnp.float32)
    keyval_w = noise(keys[6], (2, D, KV * DH), D ** -0.5, 0.1875, ((1, 8), (2, 4)), jnp.float32)
    out_w = noise(keys[7], (H * DH, D), (max(1, H * DH * 8 // SEQ_LEN)) ** -0.5, 2.0, ((0, 4), (1, 8)), jnp.float32)
    cross_query_w = noise(keys[8], (D, H * DH), D ** -0.5, 0.1875, ((0, 8), (1, 4)), jnp.float32)
    cross_keyval_w = noise(keys[9], (2, D, KV * DH), D ** -0.5, 0.1875, ((1, 8), (2, 4)), jnp.float32)
    cross_out_w = noise(keys[10], (H * DH, D), (max(1, H * DH * 8 // MEM)) ** -0.5, 1.5, ((0, 4), (1, 8)), jnp.float32)
    gateup_w = noise(keys[11], (2, D, FF), D ** -0.5, 0.1875, ((1, 8), (2, 4)), jnp.float32)
    down_w = noise(keys[12], (FF, D), FF ** -0.5, 0.109375, ((0, 4), (1, 8)), jnp.float32)
    gains = jnp.clip(1.0 + 0.1 * jax.random.normal(keys[13], (3, D), jnp.float32), 0.5, 1.5)
    rel_table = noise(keys[14], (H, BUCKETS), 1.0, 4.0, ((0, 4), (1, 8)), jnp.float32)
    query_m = noise(keys[15], (D, H * DH), (0.11 / NPARAMS ** 0.5), 0.0004272461, ((0, 8), (1, 4)), jnp.float32)
    keyval_m = noise(keys[16], (2, D, KV * DH), (0.11 / NPARAMS ** 0.5), 0.0004272461, ((1, 8), (2, 4)), jnp.float32)
    out_m = noise(keys[17], (H * DH, D), (0.027 / NPARAMS ** 0.5), 0.00010681152, ((0, 4), (1, 8)), jnp.float32)
    cross_query_m = noise(keys[18], (D, H * DH), (0.11 / NPARAMS ** 0.5), 0.0004272461, ((0, 8), (1, 4)), jnp.float32)
    cross_keyval_m = noise(keys[19], (2, D, KV * DH), (0.11 / NPARAMS ** 0.5), 0.0004272461, ((1, 8), (2, 4)), jnp.float32)
    cross_out_m = noise(keys[20], (H * DH, D), (0.022 / NPARAMS ** 0.5), 7.62939453125e-05, ((0, 4), (1, 8)), jnp.float32)
    gateup_m = noise(keys[21], (2, D, FF), (0.049 / NPARAMS ** 0.5), 0.00018310547, ((1, 8), (2, 4)), jnp.float32)
    down_m = noise(keys[22], (FF, D), (0.11 / NPARAMS ** 0.5), 0.0004272461, ((0, 4), (1, 8)), jnp.float32)
    gains_m = noise(keys[23], (3, D), (0.45 / NPARAMS ** 0.5), 0.0017089844, ((1, 8),), jnp.float32)
    rel_table_m = noise(keys[24], (H, BUCKETS), (0.45 / NPARAMS ** 0.5), 0.0017089844, ((0, 4), (1, 8)), jnp.float32)
    query_v = jnp.clip(jnp.exp(math.log(1.405077743044103e-08) - 1.3768156 * jax.random.uniform(keys[25], (D, H * DH), jnp.float32) ** level_of(keys[25], (D, H * DH), ((0, 8), (1, 4)), -0.2, 0.2)), 3.5461487080112875e-09, 1.405077743044103e-08)
    keyval_v = jnp.clip(jnp.exp(math.log(1.405077743044103e-08) - 1.3768156 * jax.random.uniform(keys[26], (2, D, KV * DH), jnp.float32) ** level_of(keys[26], (2, D, KV * DH), ((1, 8), (2, 4)), -0.2, 0.2)), 3.5461487080112875e-09, 1.405077743044103e-08)
    out_v = jnp.clip(jnp.exp(math.log(8.430466325037855e-10) - 1.370546 * jax.random.uniform(keys[27], (H * DH, D), jnp.float32) ** level_of(keys[27], (H * DH, D), ((0, 4), (1, 8)), -0.2, 0.2)), 2.1410709316604937e-10, 8.430466325037855e-10)
    cross_query_v = jnp.clip(jnp.exp(math.log(1.405077743044103e-08) - 1.3768156 * jax.random.uniform(keys[28], (D, H * DH), jnp.float32) ** level_of(keys[28], (D, H * DH), ((0, 8), (1, 4)), -0.2, 0.2)), 3.5461487080112875e-09, 1.405077743044103e-08)
    cross_keyval_v = jnp.clip(jnp.exp(math.log(1.405077743044103e-08) - 1.3768156 * jax.random.uniform(keys[29], (2, D, KV * DH), jnp.float32) ** level_of(keys[29], (2, D, KV * DH), ((1, 8), (2, 4)), -0.2, 0.2)), 3.5461487080112875e-09, 1.405077743044103e-08)
    cross_out_v = jnp.clip(jnp.exp(math.log(5.62031088335857e-10) - 1.3862944 * jax.random.uniform(keys[30], (H * DH, D), jnp.float32) ** level_of(keys[30], (H * DH, D), ((0, 4), (1, 8)), -0.2, 0.2)), 1.4050777208396426e-10, 5.62031088335857e-10)
    gateup_v = jnp.clip(jnp.exp(math.log(2.810155441679285e-09) - 1.3768156 * jax.random.uniform(keys[31], (2, D, FF), jnp.float32) ** level_of(keys[31], (2, D, FF), ((1, 8), (2, 4)), -0.2, 0.2)), 7.092297305000272e-10, 2.810155441679285e-09)
    down_v = jnp.clip(jnp.exp(math.log(1.405077743044103e-08) - 1.3768156 * jax.random.uniform(keys[32], (FF, D), jnp.float32) ** level_of(keys[32], (FF, D), ((0, 4), (1, 8)), -0.2, 0.2)), 3.5461487080112875e-09, 1.405077743044103e-08)
    gains_v = jnp.clip(jnp.exp(math.log(2.274887833664252e-07) - 1.39812884 * jax.random.uniform(keys[33], (3, D), jnp.float32) ** level_of(keys[33], (3, D), ((1, 8),), -0.2, 0.2)), 5.620310972176412e-08, 2.274887833664252e-07)
    rel_table_v = jnp.clip(jnp.exp(math.log(2.274887833664252e-07) - 1.39812884 * jax.random.uniform(keys[34], (H, BUCKETS), jnp.float32) ** level_of(keys[34], (H, BUCKETS), ((0, 4), (1, 8)), -0.2, 0.2)), 5.620310972176412e-08, 2.274887833664252e-07)
    return {"rows_in": rows_in, "memory": memory, "lengths": lengths, "mem_lengths": mem_lengths, "cotangent": cotangent, "query_w": query_w, "keyval_w": keyval_w, "out_w": out_w, "cross_query_w": cross_query_w, "cross_keyval_w": cross_keyval_w, "cross_out_w": cross_out_w, "gateup_w": gateup_w, "down_w": down_w, "gains": gains, "rel_table": rel_table, "query_m": query_m, "keyval_m": keyval_m, "out_m": out_m, "cross_query_m": cross_query_m, "cross_keyval_m": cross_keyval_m, "cross_out_m": cross_out_m, "gateup_m": gateup_m, "down_m": down_m, "gains_m": gains_m, "rel_table_m": rel_table_m, "query_v": query_v, "keyval_v": keyval_v, "out_v": out_v, "cross_query_v": cross_query_v, "cross_keyval_v": cross_keyval_v, "cross_out_v": cross_out_v, "gateup_v": gateup_v, "down_v": down_v, "gains_v": gains_v, "rel_table_v": rel_table_v}


@jax.custom_vjp
def low(v):
    return lax.optimization_barrier(v.astype(jnp.bfloat16)).astype(jnp.float32)

@jax.custom_vjp
def low_back(v):
    return v

def low_keep(v):
    return (low(v), None)

def low_pass(kept, grad):
    return (grad,)

def back_keep(v):
    return (v, None)

def back_low(kept, grad):
    return (low(grad),)
low.defvjp(low_keep, low_pass)
low_back.defvjp(back_keep, back_low)
bucket_edges = np.array([math.ceil(16.0 * 8.0 ** ((level - 16) / 16.0)) for level in range(17, 32)], dtype=np.int32)
score_scale = 0.125
masked_fill = -1e+30
norm_epsilon = 1e-06
clip_limit = 1.0
beta_one = 0.9
beta_two = 0.95
adam_epsilon = 1e-08
decay_rate = 0.1

def update_rates():
    return (D ** (-0.5), D ** (-0.5), max(1, H * DH * 8 // SEQ_LEN) ** (-0.5), D ** (-0.5), D ** (-0.5), max(1, H * DH * 8 // MEM) ** (-0.5), D ** (-0.5), FF ** (-0.5), 1.0, 0.5)

def bucket_index(offset):
    passed = lax.optimization_barrier(jnp.sum((offset[..., None] >= jnp.asarray(bucket_edges)).astype(jnp.int32), axis=-1))
    return jnp.where(offset < 16, offset, 16 + passed).astype(jnp.int32)

def bucket_onehot(seq_len, buckets):
    offsets = jnp.arange(seq_len, dtype=jnp.int32)
    levels = jnp.arange(buckets, dtype=jnp.int32)
    return (bucket_index(offsets)[:, None] == levels[None, :]).astype(jnp.float32)

def highest(left, right):
    return jnp.dot(left, right, precision=lax.Precision.HIGHEST)

def rms_scale(rows, gain):
    return rows * lax.rsqrt(lax.optimization_barrier(jnp.mean(rows * rows, axis=-1, keepdims=True)) + norm_epsilon) * gain

def attend(queries, keyval, allowed, bias):
    query_len = queries.shape[0]
    key_len = keyval.shape[1]
    kv_heads = keyval.shape[2] // DH
    groups = queries.shape[1] // DH // kv_heads
    query_heads = queries.reshape(query_len, kv_heads, groups, DH)
    key_heads = keyval[0].reshape(key_len, kv_heads, DH)
    value_heads = keyval[1].reshape(key_len, kv_heads, DH)
    raw_scores = jnp.einsum('qcgd,kcd->cgqk', query_heads, key_heads, precision=lax.Precision.HIGHEST) * score_scale
    raw_scores = raw_scores + bias
    scores = low_back(jnp.where(allowed, raw_scores, masked_fill))
    row_max = lax.optimization_barrier(jnp.max(scores, axis=-1, keepdims=True))
    exponent = jnp.exp(scores - row_max)
    attn_probs = low(exponent / lax.optimization_barrier(jnp.sum(exponent, axis=-1, keepdims=True)))
    context = low_back(low(jnp.einsum('cgqk,kcd->qcgd', attn_probs, value_heads, precision=lax.Precision.HIGHEST)))
    return context.reshape(query_len, -1)

def sequence_layer(weights, packed):
    rows, memory_rows, length, memory_length = packed
    w_query, w_keyval, w_out, w_cross_query, w_cross_keyval, w_cross_out, w_gateup, w_down, gain_low, bias_vec = weights
    seq_len = rows.shape[0]
    kv_heads = w_keyval.shape[2] // DH
    groups = w_query.shape[1] // DH // kv_heads
    normed = low(rms_scale(rows, gain_low[0]))
    queries = low_back(low(highest(normed, w_query)))
    keyval = low_back(low(jnp.einsum('ld,cde->cle', normed, w_keyval, precision=lax.Precision.HIGHEST)))
    position = jnp.arange(seq_len, dtype=jnp.int32)
    offset = position[:, None] - position[None, :]
    bias_full = jnp.take(bias_vec, jnp.clip(offset, 0, seq_len - 1), axis=1).reshape(kv_heads, groups, seq_len, seq_len)
    allowed = (offset >= 0) & (position[None, :] < length)
    context = attend(queries, keyval, allowed, bias_full)
    middle = rows + low_back(highest(context, w_out))
    normed_cross = low(rms_scale(middle, gain_low[1]))
    cross_queries = low_back(low(highest(normed_cross, w_cross_query)))
    memory_kv = low_back(low(jnp.einsum('md,cde->cme', memory_rows, w_cross_keyval, precision=lax.Precision.HIGHEST)))
    memory_allowed = (jnp.arange(memory_rows.shape[0], dtype=jnp.int32) < memory_length)[None, :]
    cross_context = attend(cross_queries, memory_kv, memory_allowed, jnp.float32(0.0))
    middle_two = middle + low_back(highest(cross_context, w_cross_out))
    normed_three = low(rms_scale(middle_two, gain_low[2]))
    gate_pre = low_back(highest(normed_three, w_gateup[0]))
    up_part = low_back(highest(normed_three, w_gateup[1]))
    hidden = low(jax.nn.gelu(gate_pre, approximate=True) * up_part)
    return middle_two + highest(hidden, w_down)

def layer_all(rows_in, memory, lengths, mem_lengths, query_w, keyval_w, out_w, cross_query_w, cross_keyval_w, cross_out_w, gateup_w, down_w, gains, rel_table):
    onehot = bucket_onehot(SEQ_LEN, BUCKETS)
    bias_vec = jnp.dot(low(rel_table), onehot.T, precision=lax.Precision.HIGHEST)
    weights = (low(query_w), low(keyval_w), low(out_w), low(cross_query_w), low(cross_keyval_w), low(cross_out_w), low(gateup_w), low(down_w), low(gains), bias_vec)

    def one_sequence(packed):
        return sequence_layer(weights, packed)
    outputs = lax.map(jax.checkpoint(one_sequence), (rows_in.reshape(-1, SEQ_LEN, rows_in.shape[1]), memory.reshape(-1, MEM, memory.shape[1]), lengths, mem_lengths))
    return outputs.reshape(rows_in.shape)

def adam_update(weight, gradient, first_moment, second_moment, factor, decay_now, rate):
    clipped = gradient * factor
    first_new = beta_one * first_moment + (1.0 - beta_one) * clipped
    second_new = beta_two * second_moment + (1.0 - beta_two) * clipped * clipped
    first_hat = first_new / (1.0 - beta_one ** STEP)
    second_hat = second_new / (1.0 - beta_two ** STEP)
    weight_new = weight - rate * (first_hat / (jnp.sqrt(second_hat) + adam_epsilon) + decay_now * weight)
    return (first_new, second_new, weight_new)

def reference(rows_in, memory, lengths, mem_lengths, cotangent, query_w, keyval_w, out_w, cross_query_w, cross_keyval_w, cross_out_w, gateup_w, down_w, gains, rel_table, query_m, keyval_m, out_m, cross_query_m, cross_keyval_m, cross_out_m, gateup_m, down_m, gains_m, rel_table_m, query_v, keyval_v, out_v, cross_query_v, cross_keyval_v, cross_out_v, gateup_v, down_v, gains_v, rel_table_v):
    params = (query_w, keyval_w, out_w, cross_query_w, cross_keyval_w, cross_out_w, gateup_w, down_w, gains, rel_table)
    firsts = (query_m, keyval_m, out_m, cross_query_m, cross_keyval_m, cross_out_m, gateup_m, down_m, gains_m, rel_table_m)
    seconds = (query_v, keyval_v, out_v, cross_query_v, cross_keyval_v, cross_out_v, gateup_v, down_v, gains_v, rel_table_v)

    def forward(rows, memory_rows, *weights):
        return layer_all(rows, memory_rows, lengths, mem_lengths, *weights)
    output, pull = jax.vjp(forward, rows_in.astype(jnp.float32), memory.astype(jnp.float32), *params)
    gradients = pull(cotangent.astype(jnp.float32))
    grad_rows = gradients[0]
    grad_memory = gradients[1]
    grad_params = gradients[2:]
    squares = jnp.zeros((), jnp.float32)
    for gradient in grad_params:
        squares = squares + jnp.sum(gradient * gradient)
    grad_norm = jnp.sqrt(squares)
    factor = clip_limit / jnp.maximum(grad_norm, clip_limit)
    rates = update_rates()
    new_firsts = []
    new_seconds = []
    new_weights = []
    for position in range(10):
        decay_now = decay_rate if position < 8 else 0.0
        first_new, second_new, weight_new = adam_update(params[position], grad_params[position], firsts[position], seconds[position], factor, decay_now, rates[position])
        new_firsts.append(first_new)
        new_seconds.append(second_new)
        new_weights.append(weight_new)
    return (output.astype(jnp.bfloat16), grad_rows, grad_memory, grad_norm, new_firsts[0], new_firsts[1], new_firsts[2], new_firsts[3], new_firsts[4], new_firsts[5], new_firsts[6], new_firsts[7], new_firsts[8], new_firsts[9], new_seconds[0], new_seconds[1], new_seconds[2], new_seconds[3], new_seconds[4], new_seconds[5], new_seconds[6], new_seconds[7], new_seconds[8], new_seconds[9], new_weights[0], new_weights[1], new_weights[2], new_weights[3], new_weights[4], new_weights[5], new_weights[6], new_weights[7], new_weights[8], new_weights[9])
```

```python
import functools
import math

import jax
import jax.numpy as jnp
import numpy as np
from jax import lax
from jax.experimental import pallas as pl
from jax.experimental.pallas import tpu as pltpu
from jax.sharding import PartitionSpec as P

D = 1024
H = 16
DH = 64
FF = 2816
SEQ_LEN = 1024
MEM = 512
STEP = 10

f32 = jnp.float32
bf16 = jnp.bfloat16

bucket_edges = np.array(
    [math.ceil(16.0 * 8.0 ** ((level - 16) / 16.0)) for level in range(17, 32)], dtype=np.int32
)
score_scale = 0.125
masked_fill = -1e30
norm_epsilon = 1e-06
clip_limit = 1.0
beta_one = 0.9
beta_two = 0.95
adam_epsilon = 1e-08
decay_rate = 0.1


def update_rates():
    return (
        D ** (-0.5),
        D ** (-0.5),
        max(1, H * DH * 8 // SEQ_LEN) ** (-0.5),
        D ** (-0.5),
        D ** (-0.5),
        max(1, H * DH * 8 // MEM) ** (-0.5),
        D ** (-0.5),
        FF ** (-0.5),
        1.0,
        0.5,
    )


def dotf(a,b,dims):
    return lax.dot_general(a,b,(dims,((),())),preferred_element_type=f32)

def place(x, src_half, dst_half):
    lane=lax.broadcasted_iota(jnp.int32,x.shape,1)
    y=x if src_half==dst_half else jnp.concatenate([x[:,64:],x[:,:64]],axis=1)
    keep=(lane<64) if dst_half==0 else (lane>=64)
    return jnp.where(keep,y,jnp.zeros_like(y))

def fwd_kernel(causal, groups, scal_ref, q_ref, k_ref, v_ref, *refs):
    if causal: strip_ref, ctx_ref, p_ref = refs
    else: ctx_ref, p_ref = refs
    length=scal_ref[0]; row0=scal_ref[1]
    R=q_ref.shape[0]; K=k_ref.shape[0]
    col=lax.broadcasted_iota(jnp.int32,(R,K),1)
    allowed=col<length
    if causal:
        row=lax.broadcasted_iota(jnp.int32,(R,K),0)+row0
        allowed=allowed&(col<=row)
    k=k_ref[...]; v=v_ref[...]
    heads=2*groups
    outs=[]
    for h in range(heads):
        u=h//groups
        qh=place(q_ref[:,(h//2)*128:(h//2)*128+128]*jnp.bfloat16(0.125),h%2,u)
        s=dotf(qh,k,((1,),(1,)))
        if causal:
            w=strip_ref.shape[-1]
            t=pltpu.roll(jnp.broadcast_to(strip_ref[h:h+1,:] if len(strip_ref.shape)==2 else strip_ref[0,h:h+1,:],(R,w)),0,1,stride=1,stride_axis=0)
            s=s+t[:,:K]
        s=jnp.where(allowed,s,masked_fill)
        m=jnp.max(s,axis=1,keepdims=True)
        e=jnp.exp(s-m)
        p=(e*(1.0/jnp.sum(e,axis=1,keepdims=True))).astype(bf16)
        p_ref[h]=p
        c=dotf(p,v,((1,),(0,))).astype(bf16)
        outs.append(place(c,u,h%2))
    for b in range(heads//2):
        ctx_ref[:,b*128:(b+1)*128]=outs[2*b]+outs[2*b+1]

def attn_fwd(q,k,v,scal,strip,causal):
    R,C=q.shape; K=k.shape[0]
    H=C//DH; KV=k.shape[1]//DH; groups=H//KV; pairs=KV//2
    hp=2*groups
    ins=[pl.BlockSpec(memory_space=pltpu.SMEM),
         pl.BlockSpec((R,hp*DH),lambda p:(0,p)),
         pl.BlockSpec((K,128),lambda p:(0,p)),
         pl.BlockSpec((K,128),lambda p:(0,p))]
    args=[scal,q,k,v]
    if causal:
        ins.append(pl.BlockSpec((1,hp,strip.shape[-1]),lambda p:(p,0,0)))
        args.append(strip.reshape(pairs,hp,-1))
    return pl.pallas_call(functools.partial(fwd_kernel,causal,groups),grid=(pairs,),
        in_specs=ins,
        out_specs=[pl.BlockSpec((R,hp*DH),lambda p:(0,p)),pl.BlockSpec((hp,R,K),lambda p:(p,0,0))],
        out_shape=[jax.ShapeDtypeStruct((R,C),bf16),jax.ShapeDtypeStruct((H,R,K),bf16)],
        compiler_params=pltpu.CompilerParams(vmem_limit_bytes=48<<20),
        name="attend_fwd")(*args)

def bwd_kernel(causal, groups, q_ref, k_ref, v_ref, p_ref, g_ref, *refs):
    if causal: flip_ref, dq_ref, dk_ref, dv_ref, diag_ref = refs
    else: dq_ref, dk_ref, dv_ref = refs
    R=q_ref.shape[0]; K=k_ref.shape[0]
    k=k_ref[...]; v=v_ref[...]
    heads=2*groups
    dqs=[]; dk=None; dv=None
    for h in range(heads):
        u=h//groups; b=(h//2)*128
        qh=place(q_ref[:,b:b+128]*jnp.bfloat16(0.125),h%2,u)
        gh=place(g_ref[:,b:b+128],h%2,u)
        pb=p_ref[h]
        p=pb.astype(f32)
        dp=dotf(gh,v,((1,),(1,)))
        pd=p*dp
        delta=jnp.sum(pd,axis=1,keepdims=True)
        gs=(pd-p*delta).astype(bf16)
        dqs.append(place((dotf(gs,k,((1,),(0,)))*0.125).astype(bf16),u,h%2))
        a=dotf(gs,qh,((0,),(0,)))
        c=dotf(pb,gh,((0,),(0,)))
        dk=a if dk is None else dk+a
        dv=c if dv is None else dv+c
        if causal:
            w=diag_ref.shape[-1]
            fl=dotf(flip_ref[...],gs,((1,),(0,)))
            fl=jnp.concatenate([fl,jnp.zeros((R,w-K),f32)],axis=1)
            diag_ref[0,h:h+1,:]=jnp.sum(pltpu.roll(fl,0,1,stride=1,stride_axis=0),axis=0,keepdims=True)
    for b in range(heads//2):
        dq_ref[:,b*128:(b+1)*128]=dqs[2*b]+dqs[2*b+1]
    dk_ref[...]=dk.astype(bf16); dv_ref[...]=dv.astype(bf16)

def attn_bwd(q,k,v,p,g,causal,W):
    R,C=q.shape; K=k.shape[0]
    H=C//DH; KV=k.shape[1]//DH; groups=H//KV; pairs=KV//2
    hp=2*groups
    ins=[pl.BlockSpec((R,hp*DH),lambda p:(0,p)),
         pl.BlockSpec((K,128),lambda p:(0,p)),
         pl.BlockSpec((K,128),lambda p:(0,p)),
         pl.BlockSpec((hp,R,K),lambda p:(p,0,0)),
         pl.BlockSpec((R,hp*DH),lambda p:(0,p))]
    args=[q,k,v,p,g]
    outs=[pl.BlockSpec((R,hp*DH),lambda p:(0,p)),pl.BlockSpec((K,128),lambda p:(0,p)),pl.BlockSpec((K,128),lambda p:(0,p))]
    shp=[jax.ShapeDtypeStruct((R,C),bf16),jax.ShapeDtypeStruct(k.shape,bf16),jax.ShapeDtypeStruct(k.shape,bf16)]
    if causal:
        ins.append(pl.BlockSpec((R,R),lambda p:(0,0)))
        args.append(jnp.asarray(np.eye(R)[::-1],bf16))
        outs.append(pl.BlockSpec((1,hp,W),lambda p:(p,0,0)))
        shp.append(jax.ShapeDtypeStruct((pairs,hp,W),f32))
    r=pl.pallas_call(functools.partial(bwd_kernel,causal,groups),grid=(pairs,),in_specs=ins,out_specs=outs,out_shape=shp,
        compiler_params=pltpu.CompilerParams(vmem_limit_bytes=48<<20),name="attend_bwd")(*args)
    return r


def bucket_onehot(offsets, buckets):
    offsets = jnp.maximum(offsets, 0)
    passed = jnp.sum((offsets[:, None] >= jnp.asarray(bucket_edges)).astype(jnp.int32), axis=-1)
    index = jnp.where(offsets < 16, offsets, 16 + passed)
    return (index[:, None] == jnp.arange(buckets, dtype=jnp.int32)[None, :]).astype(f32)


def root_of(rows):
    return lax.rsqrt(jnp.mean(rows * rows, axis=-1, keepdims=True) + norm_epsilon)


def norm_rows(rows, gain):
    return (rows * root_of(rows) * gain).astype(bf16)


def norm_back(grad, rows, gain):
    root = root_of(rows)
    scaled = rows * root
    weighted = grad * gain
    grad_rows = root * (weighted - scaled * jnp.mean(weighted * scaled, axis=-1, keepdims=True))
    return grad_rows, jnp.sum(grad * scaled, axis=0)


def ffn_kernel(x_ref, c_ref, wg_ref, wd_ref, out_ref, dx_ref, gg_ref, gd_ref):
    x = x_ref[...]
    c = c_ref[...]
    wg = wg_ref[0, 0]
    wu = wg_ref[0, 1]
    wd = wd_ref[...]
    gate = dotf(x, wg, ((1,), (0,)))
    upper = dotf(x, wu, ((1,), (0,)))
    cubic = math.sqrt(2.0 / math.pi)
    square = gate * gate
    t = jnp.tanh(cubic * gate * (1.0 + 0.044715 * square))
    half = 0.5 * (1.0 + t)
    act = gate * half
    slope = half + 0.5 * gate * (1.0 - t * t) * cubic * (1.0 + 3.0 * 0.044715 * square)
    hidden = (act * upper).astype(bf16)
    grad_hidden = dotf(c, wd, ((1,), (1,)))
    grad_gate = (grad_hidden * upper * slope).astype(bf16)
    grad_upper = (grad_hidden * act).astype(bf16)
    part = dotf(hidden, wd, ((1,), (0,)))
    back = dotf(grad_gate, wg, ((1,), (1,))) + dotf(grad_upper, wu, ((1,), (1,)))
    gd_ref[...] = dotf(hidden, c, ((0,), (0,))).astype(bf16)
    gg_ref[0, 0] = dotf(x, grad_gate, ((0,), (0,))).astype(bf16)
    gg_ref[0, 1] = dotf(x, grad_upper, ((0,), (0,))).astype(bf16)

    @pl.when(pl.program_id(0) == 0)
    def _():
        out_ref[...] = part
        dx_ref[...] = back

    @pl.when(pl.program_id(0) > 0)
    def _():
        out_ref[...] += part
        dx_ref[...] += back


def feed_forward(x, cot, w_gateup, w_down):
    rows, width = x.shape
    blocks, unused, unused_d, units = w_gateup.shape
    whole = pl.BlockSpec((rows, width), lambda i: (0, 0))
    gates = pl.BlockSpec((1, 2, width, units), lambda i: (i, 0, 0, 0))
    downs = pl.BlockSpec((units, width), lambda i: (i, 0))
    return pl.pallas_call(
        ffn_kernel,
        grid=(blocks,),
        in_specs=[whole, whole, gates, downs],
        out_specs=[whole, whole, gates, downs],
        out_shape=[
            jax.ShapeDtypeStruct((rows, width), f32),
            jax.ShapeDtypeStruct((rows, width), f32),
            jax.ShapeDtypeStruct(w_gateup.shape, bf16),
            jax.ShapeDtypeStruct(w_down.shape, bf16),
        ],
        compiler_params=pltpu.CompilerParams(vmem_limit_bytes=56 << 20),
        name="feed_forward",
    )(x, cot, w_gateup, w_down)


def mm(a, b):
    return jnp.dot(a, b, preferred_element_type=f32)


def mm_nt(a, b):
    return dotf(a, b, ((1,), (1,)))


def mm_tn(a, b):
    return dotf(a, b, ((0,), (0,)))


def gather_full(shard, dp_axis, tp_axis):
    part = lax.all_gather(shard, "tp", axis=tp_axis, tiled=True)
    return lax.all_gather(part, "dp", axis=dp_axis, tiled=True)


def scatter_sum(whole, dp_axis, tp_axis):
    part = lax.psum_scatter(whole, "dp", scatter_dimension=dp_axis, tiled=True)
    return lax.psum_scatter(part, "tp", scatter_dimension=tp_axis, tiled=True).astype(f32)


def adam_update(weight, gradient, first_moment, second_moment, factor, decay_now, rate):
    clipped = gradient * factor
    first_new = beta_one * first_moment + (1.0 - beta_one) * clipped
    second_new = beta_two * second_moment + (1.0 - beta_two) * clipped * clipped
    first_hat = first_new / (1.0 - beta_one**STEP)
    second_hat = second_new / (1.0 - beta_two**STEP)
    weight_new = weight - rate * (
        first_hat / (jnp.sqrt(second_hat) + adam_epsilon) + decay_now * weight
    )
    return (first_new, second_new, weight_new)


def per_device(
    rows_in,
    memory,
    lengths,
    mem_lengths,
    cotangent,
    query_w,
    keyval_w,
    out_w,
    cross_query_w,
    cross_keyval_w,
    cross_out_w,
    gateup_w,
    down_w,
    gains,
    rel_table,
    query_m,
    keyval_m,
    out_m,
    cross_query_m,
    cross_keyval_m,
    cross_out_m,
    gateup_m,
    down_m,
    gains_m,
    rel_table_m,
    query_v,
    keyval_v,
    out_v,
    cross_query_v,
    cross_keyval_v,
    cross_out_v,
    gateup_v,
    down_v,
    gains_v,
    rel_table_v,
):
    low = lambda w: w.astype(bf16)
    w_query = gather_full(low(query_w), 0, 1)
    w_keyval = gather_full(low(keyval_w), 1, 2)
    w_out = gather_full(low(out_w), 1, 0)
    w_cross_query = gather_full(low(cross_query_w), 0, 1)
    w_cross_keyval = gather_full(low(cross_keyval_w), 1, 2)
    w_cross_out = gather_full(low(cross_out_w), 1, 0)
    w_gateup = gather_full(low(gateup_w)[None], 2, 0)
    w_down = gather_full(low(down_w), 1, 0)
    gain_low = lax.all_gather(low(gains), "dp", axis=1, tiled=True).astype(f32)
    table_low = gather_full(low(rel_table), 1, 0)
    rows_group = lax.all_gather(rows_in, "tp", axis=0, tiled=True)
    memory_group = lax.all_gather(memory, "tp", axis=0, tiled=True)

    rows_local = rows_in.shape[0]
    key_rows = rows_group.shape[0]
    buckets = table_low.shape[1]
    own_start = lax.axis_index("tp") * rows_local
    width = key_rows + rows_local
    place_index = jnp.arange(width, dtype=jnp.int32)
    signed = jnp.where(place_index >= key_rows, place_index - width, place_index)
    strip = dotf(
        table_low, bucket_onehot(own_start - signed, buckets).astype(bf16), ((1,), (1,))
    )
    diag_onehot = bucket_onehot(own_start + rows_local - 1 - place_index, buckets)

    residual = rows_in.astype(f32)
    normed_group = norm_rows(rows_group.astype(f32), gain_low[0])
    normed = norm_rows(residual, gain_low[0])
    queries = mm(normed, w_query).astype(bf16)
    keys = mm(normed_group, w_keyval[0]).astype(bf16)
    values = mm(normed_group, w_keyval[1]).astype(bf16)
    self_scalars = jnp.stack([lengths[0], own_start.astype(jnp.int32)])
    context, probs = attn_fwd(queries, keys, values, self_scalars, strip, True)
    middle = residual + mm(context, w_out)

    normed_cross = norm_rows(middle, gain_low[1])
    cross_queries = mm(normed_cross, w_cross_query).astype(bf16)
    memory_keys = mm(memory_group, w_cross_keyval[0]).astype(bf16)
    memory_values = mm(memory_group, w_cross_keyval[1]).astype(bf16)
    cross_scalars = jnp.stack([mem_lengths[0], own_start.astype(jnp.int32)])
    cross_context, cross_probs = attn_fwd(
        cross_queries, memory_keys, memory_values, cross_scalars, None, False
    )
    middle_two = middle + mm(cross_context, w_cross_out)
    normed_three = norm_rows(middle_two, gain_low[2])

    hidden_out, grad_normed_three, grad_gateup, grad_down = feed_forward(
        normed_three, cotangent, w_gateup, w_down
    )
    block_out = (middle_two + hidden_out).astype(bf16)
    back_three, grad_gain_three = norm_back(grad_normed_three, middle_two, gain_low[2])
    grad_middle_two = cotangent.astype(f32) + back_three

    cross_branch = grad_middle_two.astype(bf16)
    grad_cross_out = mm_tn(cross_context, cross_branch).astype(bf16)
    grad_cross_context = mm_nt(cross_branch, w_cross_out).astype(bf16)
    grad_cross_queries, part_mk, part_mv = attn_bwd(
        cross_queries, memory_keys, memory_values, cross_probs, grad_cross_context, False, width
    )
    grad_memory_kv = lax.psum_scatter(
        jnp.concatenate([part_mk, part_mv], axis=1), "tp", scatter_dimension=0, tiled=True
    )
    kv_wide = part_mk.shape[1]
    grad_cross_query = mm_tn(normed_cross, grad_cross_queries).astype(bf16)
    grad_normed_cross = mm_nt(grad_cross_queries, w_cross_query)
    grad_cross_keyval = jnp.stack(
        [
            mm_tn(memory, grad_memory_kv[:, :kv_wide]).astype(bf16),
            mm_tn(memory, grad_memory_kv[:, kv_wide:]).astype(bf16),
        ]
    )
    grad_memory = mm_nt(grad_memory_kv[:, :kv_wide], w_cross_keyval[0]) + mm_nt(
        grad_memory_kv[:, kv_wide:], w_cross_keyval[1]
    )
    back_cross, grad_gain_cross = norm_back(grad_normed_cross, middle, gain_low[1])
    grad_middle = grad_middle_two + back_cross

    branch = grad_middle.astype(bf16)
    grad_out = mm_tn(context, branch).astype(bf16)
    grad_context = mm_nt(branch, w_out).astype(bf16)
    grad_queries, part_k, part_v, diagonals = attn_bwd(
        queries, keys, values, probs, grad_context, True, width
    )
    grad_keyvals = lax.psum_scatter(
        jnp.concatenate([part_k, part_v], axis=1), "tp", scatter_dimension=0, tiled=True
    )
    grad_table = jnp.dot(
        diagonals.reshape(-1, width), diag_onehot, precision=lax.Precision.HIGHEST
    )
    grad_query = mm_tn(normed, grad_queries).astype(bf16)
    grad_keyval = jnp.stack(
        [
            mm_tn(normed, grad_keyvals[:, :kv_wide]).astype(bf16),
            mm_tn(normed, grad_keyvals[:, kv_wide:]).astype(bf16),
        ]
    )
    grad_normed = (
        mm_nt(grad_queries, w_query)
        + mm_nt(grad_keyvals[:, :kv_wide], w_keyval[0])
        + mm_nt(grad_keyvals[:, kv_wide:], w_keyval[1])
    )
    back_one, grad_gain_one = norm_back(grad_normed, residual, gain_low[0])
    grad_rows = grad_middle + back_one

    reduced = (
        scatter_sum(grad_query, 0, 1),
        scatter_sum(grad_keyval, 1, 2),
        scatter_sum(grad_out, 1, 0),
        scatter_sum(grad_cross_query, 0, 1),
        scatter_sum(grad_cross_keyval, 1, 2),
        scatter_sum(grad_cross_out, 1, 0),
        scatter_sum(grad_gateup, 2, 0)[0],
        scatter_sum(grad_down, 1, 0),
    )
    squares = jnp.zeros((), f32)
    for piece in reduced:
        squares = squares + jnp.sum(piece * piece)
    gain_terms = jnp.stack([grad_gain_one, grad_gain_cross, grad_gain_three])
    squares_all, gains_full, table_full = lax.psum((squares, gain_terms, grad_table), ("dp", "tp"))
    grad_norm = jnp.sqrt(
        squares_all + jnp.sum(gains_full * gains_full) + jnp.sum(table_full * table_full)
    )
    factor = clip_limit / jnp.maximum(grad_norm, clip_limit)
    gains_grad = lax.dynamic_slice_in_dim(
        gains_full, lax.axis_index("dp") * gains.shape[1], gains.shape[1], 1
    )
    table_grad = lax.dynamic_slice(
        table_full,
        (
            lax.axis_index("tp") * rel_table.shape[0],
            lax.axis_index("dp") * rel_table.shape[1],
        ),
        rel_table.shape,
    )
    grad_list = reduced + (gains_grad, table_grad)
    params = (
        query_w,
        keyval_w,
        out_w,
        cross_query_w,
        cross_keyval_w,
        cross_out_w,
        gateup_w,
        down_w,
        gains,
        rel_table,
    )
    firsts = (
        query_m,
        keyval_m,
        out_m,
        cross_query_m,
        cross_keyval_m,
        cross_out_m,
        gateup_m,
        down_m,
        gains_m,
        rel_table_m,
    )
    seconds = (
        query_v,
        keyval_v,
        out_v,
        cross_query_v,
        cross_keyval_v,
        cross_out_v,
        gateup_v,
        down_v,
        gains_v,
        rel_table_v,
    )
    rates = update_rates()
    new_firsts = []
    new_seconds = []
    new_weights = []
    for position in range(10):
        decay_now = decay_rate if position < 8 else 0.0
        first_new, second_new, weight_new = adam_update(
            params[position],
            grad_list[position],
            firsts[position],
            seconds[position],
            factor,
            decay_now,
            rates[position],
        )
        new_firsts.append(first_new)
        new_seconds.append(second_new)
        new_weights.append(weight_new)
    return (
        block_out,
        grad_rows,
        grad_memory,
        grad_norm,
        new_firsts[0],
        new_firsts[1],
        new_firsts[2],
        new_firsts[3],
        new_firsts[4],
        new_firsts[5],
        new_firsts[6],
        new_firsts[7],
        new_firsts[8],
        new_firsts[9],
        new_seconds[0],
        new_seconds[1],
        new_seconds[2],
        new_seconds[3],
        new_seconds[4],
        new_seconds[5],
        new_seconds[6],
        new_seconds[7],
        new_seconds[8],
        new_seconds[9],
        new_weights[0],
        new_weights[1],
        new_weights[2],
        new_weights[3],
        new_weights[4],
        new_weights[5],
        new_weights[6],
        new_weights[7],
        new_weights[8],
        new_weights[9],
    )


def solution(mesh):
    return jax.shard_map(
        per_device,
        mesh=mesh,
        in_specs=(
            P(("dp", "tp"), None),
            P(("dp", "tp"), None),
            P("dp"),
            P("dp"),
            P(("dp", "tp"), None),
            P("dp", "tp"),
            P(None, "dp", "tp"),
            P("tp", "dp"),
            P("dp", "tp"),
            P(None, "dp", "tp"),
            P("tp", "dp"),
            P(None, "dp", "tp"),
            P("tp", "dp"),
            P(None, "dp"),
            P("tp", "dp"),
            P("dp", "tp"),
            P(None, "dp", "tp"),
            P("tp", "dp"),
            P("dp", "tp"),
            P(None, "dp", "tp"),
            P("tp", "dp"),
            P(None, "dp", "tp"),
            P("tp", "dp"),
            P(None, "dp"),
            P("tp", "dp"),
            P("dp", "tp"),
            P(None, "dp", "tp"),
            P("tp", "dp"),
            P("dp", "tp"),
            P(None, "dp", "tp"),
            P("tp", "dp"),
            P(None, "dp", "tp"),
            P("tp", "dp"),
            P(None, "dp"),
            P("tp", "dp"),
        ),
        out_specs=(
            P(("dp", "tp"), None),
            P(("dp", "tp"), None),
            P(("dp", "tp"), None),
            P(),
            P("dp", "tp"),
            P(None, "dp", "tp"),
            P("tp", "dp"),
            P("dp", "tp"),
            P(None, "dp", "tp"),
            P("tp", "dp"),
            P(None, "dp", "tp"),
            P("tp", "dp"),
            P(None, "dp"),
            P("tp", "dp"),
            P("dp", "tp"),
            P(None, "dp", "tp"),
            P("tp", "dp"),
            P("dp", "tp"),
            P(None, "dp", "tp"),
            P("tp", "dp"),
            P(None, "dp", "tp"),
            P("tp", "dp"),
            P(None, "dp"),
            P("tp", "dp"),
            P("dp", "tp"),
            P(None, "dp", "tp"),
            P("tp", "dp"),
            P("dp", "tp"),
            P(None, "dp", "tp"),
            P("tp", "dp"),
            P(None, "dp", "tp"),
            P("tp", "dp"),
            P(None, "dp"),
            P("tp", "dp"),
        ),
        check_vma=False,
    )
```

```python
import functools
import math

import jax
import jax.numpy as jnp
import numpy as np
from jax import lax
from jax.experimental import pallas as pl
from jax.experimental.pallas import tpu as pltpu
from jax.sharding import PartitionSpec as P

D = 1024
H = 16
DH = 64
FF = 2816
SEQ_LEN = 1024
MEM = 512
STEP = 10

f32 = jnp.float32
bf16 = jnp.bfloat16

bucket_edges = np.array(
    [math.ceil(16.0 * 8.0 ** ((level - 16) / 16.0)) for level in range(17, 32)], dtype=np.int32
)
score_scale = 0.125
masked_fill = -1e30
norm_epsilon = 1e-06
clip_limit = 1.0
beta_one = 0.9
beta_two = 0.95
adam_epsilon = 1e-08
decay_rate = 0.1


def update_rates():
    return (
        D ** (-0.5),
        D ** (-0.5),
        max(1, H * DH * 8 // SEQ_LEN) ** (-0.5),
        D ** (-0.5),
        D ** (-0.5),
        max(1, H * DH * 8 // MEM) ** (-0.5),
        D ** (-0.5),
        FF ** (-0.5),
        1.0,
        0.5,
    )


def dotf(a,b,dims):
    return lax.dot_general(a,b,(dims,((),())),preferred_element_type=f32)

def place(x, src_half, dst_half):
    lane=lax.broadcasted_iota(jnp.int32,x.shape,1)
    y=x if src_half==dst_half else jnp.concatenate([x[:,64:],x[:,:64]],axis=1)
    keep=(lane<64) if dst_half==0 else (lane>=64)
    return jnp.where(keep,y,jnp.zeros_like(y))

def fwd_kernel(causal, groups, scal_ref, q_ref, k_ref, v_ref, *refs):
    if causal: strip_ref, ctx_ref, p_ref = refs
    else: ctx_ref, p_ref = refs
    length=scal_ref[0]; row0=scal_ref[1]
    R=q_ref.shape[0]; K=k_ref.shape[0]
    col=lax.broadcasted_iota(jnp.int32,(R,K),1)
    allowed=col<length
    if causal:
        row=lax.broadcasted_iota(jnp.int32,(R,K),0)+row0
        allowed=allowed&(col<=row)
    k=k_ref[...]; v=v_ref[...]
    heads=2*groups
    outs=[]
    for h in range(heads):
        u=h//groups
        qh=place(q_ref[:,(h//2)*128:(h//2)*128+128]*jnp.bfloat16(0.125),h%2,u)
        s=dotf(qh,k,((1,),(1,)))
        if causal:
            w=strip_ref.shape[-1]
            t=pltpu.roll(jnp.broadcast_to(strip_ref[h:h+1,:] if len(strip_ref.shape)==2 else strip_ref[0,h:h+1,:],(R,w)),0,1,stride=1,stride_axis=0)
            s=s+t[:,:K]
        s=jnp.where(allowed,s,masked_fill)
        m=jnp.max(s,axis=1,keepdims=True)
        e=jnp.exp(s-m)
        p=(e*(1.0/jnp.sum(e,axis=1,keepdims=True))).astype(bf16)
        p_ref[h]=p
        c=dotf(p,v,((1,),(0,))).astype(bf16)
        outs.append(place(c,u,h%2))
    for b in range(heads//2):
        ctx_ref[:,b*128:(b+1)*128]=outs[2*b]+outs[2*b+1]

def attn_fwd(q,k,v,scal,strip,causal):
    R,C=q.shape; K=k.shape[0]
    H=C//DH; KV=k.shape[1]//DH; groups=H//KV; pairs=KV//2
    hp=2*groups
    ins=[pl.BlockSpec(memory_space=pltpu.SMEM),
         pl.BlockSpec((R,hp*DH),lambda p:(0,p)),
         pl.BlockSpec((K,128),lambda p:(0,p)),
         pl.BlockSpec((K,128),lambda p:(0,p))]
    args=[scal,q,k,v]
    if causal:
        ins.append(pl.BlockSpec((1,hp,strip.shape[-1]),lambda p:(p,0,0)))
        args.append(strip.reshape(pairs,hp,-1))
    return pl.pallas_call(functools.partial(fwd_kernel,causal,groups),grid=(pairs,),
        in_specs=ins,
        out_specs=[pl.BlockSpec((R,hp*DH),lambda p:(0,p)),pl.BlockSpec((hp,R,K),lambda p:(p,0,0))],
        out_shape=[jax.ShapeDtypeStruct((R,C),bf16),jax.ShapeDtypeStruct((H,R,K),bf16)],
        compiler_params=pltpu.CompilerParams(vmem_limit_bytes=48<<20),
        name="attend_fwd")(*args)

def bwd_kernel(causal, groups, q_ref, k_ref, v_ref, p_ref, g_ref, *refs):
    if causal: flip_ref, dq_ref, dk_ref, dv_ref, diag_ref = refs
    else: dq_ref, dk_ref, dv_ref = refs
    R=q_ref.shape[0]; K=k_ref.shape[0]
    k=k_ref[...]; v=v_ref[...]
    heads=2*groups
    dqs=[]; dk=None; dv=None
    for h in range(heads):
        u=h//groups; b=(h//2)*128
        qh=place(q_ref[:,b:b+128]*jnp.bfloat16(0.125),h%2,u)
        gh=place(g_ref[:,b:b+128],h%2,u)
        pb=p_ref[h]
        p=pb.astype(f32)
        dp=dotf(gh,v,((1,),(1,)))
        pd=p*dp
        delta=jnp.sum(pd,axis=1,keepdims=True)
        gs=(pd-p*delta).astype(bf16)
        dqs.append(place((dotf(gs,k,((1,),(0,)))*0.125).astype(bf16),u,h%2))
        a=dotf(gs,qh,((0,),(0,)))
        c=dotf(pb,gh,((0,),(0,)))
        dk=a if dk is None else dk+a
        dv=c if dv is None else dv+c
        if causal:
            w=diag_ref.shape[-1]
            fl=dotf(flip_ref[...],gs,((1,),(0,)))
            fl=jnp.concatenate([fl,jnp.zeros((R,w-K),f32)],axis=1)
            diag_ref[0,h:h+1,:]=jnp.sum(pltpu.roll(fl,0,1,stride=1,stride_axis=0),axis=0,keepdims=True)
    for b in range(heads//2):
        dq_ref[:,b*128:(b+1)*128]=dqs[2*b]+dqs[2*b+1]
    dk_ref[...]=dk.astype(bf16); dv_ref[...]=dv.astype(bf16)

def attn_bwd(q,k,v,p,g,causal,W):
    R,C=q.shape; K=k.shape[0]
    H=C//DH; KV=k.shape[1]//DH; groups=H//KV; pairs=KV//2
    hp=2*groups
    ins=[pl.BlockSpec((R,hp*DH),lambda p:(0,p)),
         pl.BlockSpec((K,128),lambda p:(0,p)),
         pl.BlockSpec((K,128),lambda p:(0,p)),
         pl.BlockSpec((hp,R,K),lambda p:(p,0,0)),
         pl.BlockSpec((R,hp*DH),lambda p:(0,p))]
    args=[q,k,v,p,g]
    outs=[pl.BlockSpec((R,hp*DH),lambda p:(0,p)),pl.BlockSpec((K,128),lambda p:(0,p)),pl.BlockSpec((K,128),lambda p:(0,p))]
    shp=[jax.ShapeDtypeStruct((R,C),bf16),jax.ShapeDtypeStruct(k.shape,bf16),jax.ShapeDtypeStruct(k.shape,bf16)]
    if causal:
        ins.append(pl.BlockSpec((R,R),lambda p:(0,0)))
        args.append(jnp.asarray(np.eye(R)[::-1],bf16))
        outs.append(pl.BlockSpec((1,hp,W),lambda p:(p,0,0)))
        shp.append(jax.ShapeDtypeStruct((pairs,hp,W),f32))
    r=pl.pallas_call(functools.partial(bwd_kernel,causal,groups),grid=(pairs,),in_specs=ins,out_specs=outs,out_shape=shp,
        compiler_params=pltpu.CompilerParams(vmem_limit_bytes=48<<20),name="attend_bwd")(*args)
    return r


MESH = pl.DeviceIdType.MESH


def neighbour(kind):
    dp = lax.axis_index("dp")
    tp = lax.axis_index("tp")
    if kind == "core":
        return (dp ^ 1, tp)
    if kind == "x":
        return (dp ^ 2, tp)
    if kind == "y":
        return (dp ^ 4, tp)
    if kind == "up":
        return (dp, tp + 1)
    if kind == "down":
        return (dp, tp - 1)


class Row:
    def __init__(self, lead, dp_part, tp_part, tp_size):
        self.lead = lead
        self.dp_part = dp_part
        self.tp_part = tp_part
        self.full = lead + (dp_part * 8, tp_part * tp_size)
        self.slab_shape = lead + (dp_part, tp_part * tp_size)
        self.shard = lead + (dp_part, tp_part)
        self.half_shape = lead + (dp_part, tp_part * (tp_size // 2))
        self.tp_size = tp_size

    def index(self, start, count):
        return (slice(None),) * len(self.lead) + (
            slice(None),
            pl.ds(pl.multiple_of(start * self.tp_part, self.tp_part), count * self.tp_part),
        )

    def one(self, start):
        return self.index(start, 1)

    def of(self, ref, dp):
        rows = pl.ds(pl.multiple_of(dp * self.dp_part, self.dp_part), self.dp_part)
        return ref.at[(slice(None),) * len(self.lead) + (rows, slice(None))]

    def part(self, ref, dp, start, count):
        rows = pl.ds(pl.multiple_of(dp * self.dp_part, self.dp_part), self.dp_part)
        cols = pl.ds(pl.multiple_of(start * self.tp_part, self.tp_part), count * self.tp_part)
        return ref.at[(slice(None),) * len(self.lead) + (rows, cols)]


class Column:
    def __init__(self, dp_part, tp_part, tp_size):
        self.dp_part = dp_part
        self.tp_part = tp_part
        self.full = (tp_part * tp_size, dp_part * 8)
        self.slab_shape = (tp_part * tp_size, dp_part)
        self.shard = (tp_part, dp_part)
        self.half_shape = (tp_part * (tp_size // 2), dp_part)
        self.tp_size = tp_size

    def index(self, start, count):
        return (
            pl.ds(pl.multiple_of(start * self.tp_part, self.tp_part), count * self.tp_part),
            slice(None),
        )

    def one(self, start):
        return self.index(start, 1)

    def of(self, ref, dp):
        return self.part(ref, dp, 0, self.tp_size)

    def part(self, ref, dp, start, count):
        cols = pl.ds(pl.multiple_of(dp * self.dp_part, self.dp_part), self.dp_part)
        rows = pl.ds(pl.multiple_of(start * self.tp_part, self.tp_part), count * self.tp_part)
        return ref.at[rows, cols]


class Block:
    def __init__(self, dp_part, tp_part, tp_size):
        self.dp_part = dp_part
        self.full = (tp_size, dp_part * 8, tp_part)
        self.slab_shape = (tp_size, dp_part, tp_part)
        self.shard = (dp_part, tp_part)
        self.half_shape = (tp_size // 2, dp_part, tp_part)
        self.tp_size = tp_size

    def index(self, start, count):
        return (pl.ds(start, count),)

    def one(self, start):
        return (start,)

    def of(self, ref, dp):
        return self.part(ref, dp, 0, self.tp_size)

    def part(self, ref, dp, start, count):
        rows = pl.ds(pl.multiple_of(dp * self.dp_part, self.dp_part), self.dp_part)
        return ref.at[start if count == 1 else pl.ds(start, count), rows]


def when(condition, action):
    pl.when(condition)(action)


def copy_to(src, dst, send_sem, recv_sem, kind):
    return pltpu.make_async_remote_copy(
        src, dst, send_sem, recv_sem, device_id=neighbour(kind), device_id_type=MESH
    )


def greet(tp_size, reach):
    dp = lax.axis_index("dp")
    tp = lax.axis_index("tp")
    barrier = pltpu.get_barrier_semaphore()
    for kind in ("core", "x", "y"):
        pl.semaphore_signal(barrier, inc=1, device_id=neighbour(kind), device_id_type=MESH)

    peers = 3
    for d in range(1, reach + 1):
        above = tp + d < tp_size
        below = tp >= d

        @pl.when(above)
        def _(d=d):
            pl.semaphore_signal(barrier, inc=1, device_id=(dp, tp + d), device_id_type=MESH)

        @pl.when(below)
        def _(d=d):
            pl.semaphore_signal(barrier, inc=1, device_id=(dp, tp - d), device_id_type=MESH)

        peers = peers + above.astype(jnp.int32) + below.astype(jnp.int32)

    pl.semaphore_wait(barrier, peers)


def gather_kernel(specs, plane, tp_size, *refs):
    count = len(specs)
    ins = refs[:count]
    outs = refs[count : 2 * count]
    local_sem, z_send, z_recv, p_send, p_recv = refs[2 * count :]
    dp = lax.axis_index("dp")
    tp = lax.axis_index("tp")
    greet(tp_size, 2)

    def own(k):
        return pltpu.make_async_copy(ins[k], specs[k].part(outs[k], dp, tp, 1), local_sem.at[k])

    def way(k, d, sign):
        slot = 0 if sign > 0 else 1
        return pltpu.make_async_remote_copy(
            ins[k],
            specs[k].part(outs[k], dp, tp, 1),
            z_send.at[k, slot, d - 1],
            z_recv.at[k, slot, d - 1],
            device_id=(dp, tp + sign * d),
            device_id_type=MESH,
        )

    def onward(k, sign):
        slot = 0 if sign > 0 else 1
        piece = specs[k].part(outs[k], dp, tp - 2 * sign, 1)
        return pltpu.make_async_remote_copy(
            piece,
            piece,
            z_send.at[k, slot, 2],
            z_recv.at[k, slot, 2],
            device_id=(dp, tp + sign),
            device_id_type=MESH,
        )

    def has(d, sign):
        return (tp + d < tp_size) if sign > 0 else (tp >= d)

    def z_start(k):
        own(k).start()
        for sign in (1, -1):
            for d in (2, 1):
                when(has(d, sign), lambda d=d, sign=sign: way(k, d, sign).start())

    def relays(sign):
        return has(2, -sign) & has(1, sign)

    def z_relay(k):
        for sign in (1, -1):

            def act(sign=sign):
                way(k, 2, sign).wait_recv()
                onward(k, sign).start()

            when(relays(sign), act)

    def z_wait(k):
        for sign in (1, -1):
            when(has(1, -sign), lambda sign=sign: way(k, 1, sign).wait_recv())
            when(
                has(2, -sign) & jnp.logical_not(relays(sign)),
                lambda sign=sign: way(k, 2, sign).wait_recv(),
            )
            when(has(3, -sign), lambda sign=sign: onward(k, sign).wait_recv())

    half = tp_size // 2

    def slab(k, who, slot, kind):
        piece = specs[k].of(outs[k], who)
        return copy_to(piece, piece, p_send.at[k, slot], p_recv.at[k, slot], kind)

    def halves(k, who, h, slot, kind):
        piece = specs[k].part(outs[k], who, h * half, half)
        return copy_to(piece, piece, p_send.at[k, slot], p_recv.at[k, slot], kind)

    def plane_start(k):
        own(k).wait()
        z_wait(k)
        if plane[k]:
            slab(k, dp, 0, "x").start()
            slab(k, dp, 1, "y").start()
            slab(k, dp, 2, "core").start()

    def plane_relay(k):
        if plane[k]:
            slab(k, dp ^ 2, 0, "x").wait_recv()
            halves(k, dp ^ 2, 0, 3, "y").start()
            slab(k, dp ^ 4, 1, "y").wait_recv()
            halves(k, dp ^ 4, 1, 4, "x").start()
            slab(k, dp ^ 2, 5, "core").start()
            slab(k, dp ^ 4, 6, "core").start()

    def plane_last(k):
        if plane[k]:
            halves(k, dp ^ 6, 0, 3, "y").wait_recv()
            halves(k, dp ^ 6, 0, 7, "core").start()
            halves(k, dp ^ 6, 1, 4, "x").wait_recv()
            halves(k, dp ^ 6, 1, 8, "core").start()

    def finish(k):
        for sign in (1, -1):
            for d in (1, 2):
                when(has(d, sign), lambda d=d, sign=sign: way(k, d, sign).wait_send())
            when(relays(sign), lambda sign=sign: onward(k, sign).wait_send())
        if plane[k]:
            slab(k, dp, 0, "x").wait_send()
            slab(k, dp, 1, "y").wait_send()
            slab(k, dp, 2, "core").wait()
            halves(k, dp ^ 2, 0, 3, "y").wait_send()
            halves(k, dp ^ 4, 1, 4, "x").wait_send()
            slab(k, dp ^ 2, 5, "core").wait()
            slab(k, dp ^ 4, 6, "core").wait()
            halves(k, dp ^ 6, 0, 7, "core").wait()
            halves(k, dp ^ 6, 1, 8, "core").wait()

    stages = ((z_start, 0), (z_relay, 1), (plane_start, 2), (plane_relay, 4), (plane_last, 5))
    for step in range(count + stages[-1][1]):
        for stage, late in stages:
            if 0 <= step - late < count:
                stage(step - late)
    for k in range(count):
        finish(k)


def gather_all(shards, specs, plane, tp_size):
    count = len(specs)
    return pl.pallas_call(
        functools.partial(gather_kernel, specs, plane, tp_size),
        in_specs=[pl.BlockSpec(memory_space=pl.ANY)] * count,
        out_specs=[pl.BlockSpec(memory_space=pl.ANY)] * count,
        out_shape=[
            jax.ShapeDtypeStruct(spec.full if flag else spec.slab_shape, shard.dtype)
            for spec, flag, shard in zip(specs, plane, shards)
        ],
        scratch_shapes=[
            pltpu.SemaphoreType.DMA((count,)),
            pltpu.SemaphoreType.DMA((count, 2, 3)),
            pltpu.SemaphoreType.DMA((count, 2, 3)),
            pltpu.SemaphoreType.DMA((count, 9)),
            pltpu.SemaphoreType.DMA((count, 9)),
        ],
        compiler_params=pltpu.CompilerParams(collective_id=1, has_side_effects=True),
        name="gather_all",
    )(*shards)


class Rows:
    def __init__(self, tp_part, columns, tp_size):
        self.tp_part = tp_part
        self.slab_shape = (tp_part * tp_size, columns)
        self.full = self.slab_shape
        self.shard = (tp_part, columns)

    def part(self, ref, dp, start, count):
        return ref.at[pl.ds(pl.multiple_of(start * self.tp_part, self.tp_part), count * self.tp_part)]


def add_views(dst, dst_index, sources):
    target = dst.at[dst_index]
    shape = target.shape
    lead = shape[:-2]
    rows = shape[-2]
    chunk = 64 if rows % 64 == 0 else 16
    for outer in np.ndindex(*lead):

        def body(i, unused, outer=outer):
            here = outer + (pl.ds(pl.multiple_of(i * chunk, chunk), chunk), slice(None))
            total = target[here].astype(f32)
            for source in sources:
                total = total + source[here].astype(f32)
            target[here] = total.astype(bf16)
            return unused

        lax.fori_loop(0, rows // chunk, body, 0)


def reduce_kernel(specs, tp_size, *refs):
    count = len(specs)
    ins = refs[:count]
    small_in = refs[count]
    outs = refs[count + 1 : 2 * count + 1]
    small_out = refs[2 * count + 1]
    norm_out = refs[2 * count + 2]
    scratch = refs[2 * count + 3 :]
    own = scratch[0:count]
    other = scratch[count : 2 * count]
    half_x = scratch[2 * count : 3 * count]
    half_y = scratch[3 * count : 4 * count]
    from_x = scratch[4 * count : 5 * count]
    from_y = scratch[5 * count : 6 * count]
    from_z = scratch[6 * count : 7 * count]
    small_acc, small_got, square_acc, square_all, square_got = scratch[7 * count : 7 * count + 5]
    load_sem, c_send, c_recv, p_send, p_recv, z_send, z_recv, s_send, s_recv = scratch[7 * count + 5 :]
    dp = lax.axis_index("dp")
    tp = lax.axis_index("tp")
    greet(tp_size, tp_size - 1)
    half = tp_size // 2

    def load(k, j):
        return pltpu.make_async_copy(specs[k].of(ins[k], dp ^ (2 * j)), own[k].at[j], load_sem.at[k, j])

    def to_core(k, j):
        return copy_to(
            specs[k].of(ins[k], dp ^ (2 * j) ^ 1), other[k].at[j], c_send.at[k, j], c_recv.at[k, j], "core"
        )

    def start(k):
        for j in (3, 2, 1, 0):
            to_core(k, j).start()
            load(k, j).start()

    def send_half(k, h):
        piece = own[k].at[(3,) + specs[k].index(h * half, half)]
        return copy_to(
            piece, (half_x, half_y)[h][k], p_send.at[k, h], p_recv.at[k, h], ("x", "y")[h]
        )

    def send_slab(k, j):
        return copy_to(
            own[k].at[j],
            (from_x, from_y)[j - 1][k],
            p_send.at[k, j + 1],
            p_recv.at[k, j + 1],
            ("x", "y")[j - 1],
        )

    def cores(k):
        for j in (3, 2, 1, 0):
            to_core(k, j).wait_recv()
            load(k, j).wait()
            add_views(own[k], (j,), [other[k].at[j]])
            if j == 3:
                send_half(k, 0).start()
                send_half(k, 1).start()

    def halves(k):
        send_half(k, 1).wait_recv()
        add_views(own[k], (1,) + specs[k].index(half, half), [half_y[k]])
        send_slab(k, 1).start()
        send_half(k, 0).wait_recv()
        add_views(own[k], (2,) + specs[k].index(0, half), [half_x[k]])
        send_slab(k, 2).start()

    def to_z(k, offset):
        target = lax.rem(tp + offset, tp_size)
        piece = own[k].at[(0,) + specs[k].one(target)]
        return pltpu.make_async_remote_copy(
            piece,
            from_z[k].at[offset - 1],
            z_send.at[k, offset - 1],
            z_recv.at[k, offset - 1],
            device_id=(dp, target),
            device_id_type=MESH,
        )

    def slabs(k):
        send_slab(k, 1).wait_recv()
        send_slab(k, 2).wait_recv()
        add_views(own[k], (0,), [from_x[k], from_y[k]])
        for offset in range(1, tp_size):
            to_z(k, offset).start()

    def last(k):
        for offset in range(1, tp_size):
            to_z(k, offset).wait_recv()
        shape = specs[k].shard
        lead = shape[:-2]
        rows = shape[-2]
        chunk = 64 if rows % 64 == 0 else 16
        mine = own[k].at[(0,) + specs[k].one(tp)]
        for outer in np.ndindex(*lead):

            def body(i, squares, outer=outer):
                here = outer + (pl.ds(pl.multiple_of(i * chunk, chunk), chunk), slice(None))
                total = mine[here].astype(f32)
                for offset in range(1, tp_size):
                    total = total + from_z[k][(offset - 1,) + here].astype(f32)
                outs[k][here] = total
                squared = jnp.sum((total * total).reshape(chunk // 8, 8, -1), axis=0)
                return squares + jnp.sum(squared, axis=1, keepdims=True)

            square_acc[...] += jnp.broadcast_to(
                lax.fori_loop(0, rows // chunk, body, jnp.zeros((8, 1), f32)), square_acc.shape
            )

    def exchange(acc, got, base):
        partners = [(dp ^ 1, tp), (dp ^ 2, tp), (dp ^ 4, tp), (dp, tp ^ 1), (dp, tp ^ 2)]

        def step(i):
            return pltpu.make_async_remote_copy(
                acc.at[i],
                got.at[i],
                s_send.at[base + i],
                s_recv.at[base + i],
                device_id=partners[i],
                device_id_type=MESH,
            )

        def run(i):
            step(i).wait_recv()
            acc[i + 1] = acc[i] + got[i]
            if i < 4:
                step(i + 1).start()

        return step, run

    small_step, small_run = exchange(small_acc, small_got, 0)
    square_step, square_run = exchange(square_all, square_got, 5)
    small_acc[0] = small_in[...]
    small_step(0).start()
    square_acc[...] = jnp.zeros(square_acc.shape, f32)
    for k in range(count):
        start(k)
    stages = ((cores, 0), (halves, 1), (slabs, 2), (last, 3))
    for step in range(count + stages[-1][1]):
        for stage, late in reversed(stages):
            if 0 <= step - late < count:
                stage(step - late)
        if step < 5:
            small_run(step)
    small_out[...] = small_acc[5]
    square_all[0] = square_acc[...]
    square_step(0).start()
    for i in range(5):
        square_run(i)
    norm_out[...] = square_all[5]
    for i in range(5):
        small_step(i).wait_send()
        square_step(i).wait_send()
    for k in range(count):
        for j in range(4):
            to_core(k, j).wait_send()
        for h in range(2):
            send_half(k, h).wait_send()
            send_slab(k, h + 1).wait_send()
        for offset in range(1, tp_size):
            to_z(k, offset).wait_send()


def reduce_all(wholes, small, specs, tp_size):
    count = len(specs)
    slab = lambda spec, lead: pltpu.VMEM(lead + spec.slab_shape, bf16)
    part = lambda spec: pltpu.VMEM(spec.half_shape, bf16)
    scratch = [slab(spec, (4,)) for spec in specs]
    scratch += [slab(spec, (4,)) for spec in specs]
    scratch += [part(spec) for spec in specs] * 2
    scratch += [slab(spec, ()) for spec in specs] * 2
    scratch += [pltpu.VMEM((tp_size - 1,) + spec.shard, bf16) for spec in specs]
    scratch += [
        pltpu.VMEM((6,) + small.shape, f32),
        pltpu.VMEM((5,) + small.shape, f32),
        pltpu.VMEM((8, 128), f32),
        pltpu.VMEM((6, 8, 128), f32),
        pltpu.VMEM((5, 8, 128), f32),
    ]
    sems = lambda *shape: pltpu.SemaphoreType.DMA(shape)
    scratch += [
        sems(count, 4),
        sems(count, 4),
        sems(count, 4),
        sems(count, 4),
        sems(count, 4),
        sems(count, tp_size - 1),
        sems(count, tp_size - 1),
        sems(10),
        sems(10),
    ]
    vmem = pl.BlockSpec(memory_space=pltpu.VMEM)
    return pl.pallas_call(
        functools.partial(reduce_kernel, specs, tp_size),
        in_specs=[pl.BlockSpec(memory_space=pl.ANY)] * count + [vmem],
        out_specs=[vmem] * (count + 2),
        out_shape=[jax.ShapeDtypeStruct(spec.shard, f32) for spec in specs]
        + [jax.ShapeDtypeStruct(small.shape, f32), jax.ShapeDtypeStruct((8, 128), f32)],
        scratch_shapes=scratch,
        compiler_params=pltpu.CompilerParams(
            collective_id=2, has_side_effects=True, vmem_limit_bytes=60 << 20
        ),
        name="reduce_all",
    )(*wholes, small)


def bucket_onehot(offsets, buckets):
    offsets = jnp.maximum(offsets, 0)
    passed = jnp.sum((offsets[:, None] >= jnp.asarray(bucket_edges)).astype(jnp.int32), axis=-1)
    index = jnp.where(offsets < 16, offsets, 16 + passed)
    return (index[:, None] == jnp.arange(buckets, dtype=jnp.int32)[None, :]).astype(f32)


def root_of(rows):
    return lax.rsqrt(jnp.mean(rows * rows, axis=-1, keepdims=True) + norm_epsilon)


def norm_rows(rows, gain):
    return (rows * root_of(rows) * gain).astype(bf16)


def norm_back(grad, rows, gain):
    root = root_of(rows)
    scaled = rows * root
    weighted = grad * gain
    grad_rows = root * (weighted - scaled * jnp.mean(weighted * scaled, axis=-1, keepdims=True))
    return grad_rows, jnp.sum(grad * scaled, axis=0)


def ffn_kernel(x_ref, c_ref, wg_ref, wu_ref, wd_ref, out_ref, dx_ref, gg_ref, gu_ref, gd_ref):
    x = x_ref[...]
    c = c_ref[...]
    wg = wg_ref[0]
    wu = wu_ref[0]
    wd = wd_ref[...]
    gate = dotf(x, wg, ((1,), (0,)))
    upper = dotf(x, wu, ((1,), (0,)))
    cubic = math.sqrt(2.0 / math.pi)
    square = gate * gate
    t = jnp.tanh(cubic * gate * (1.0 + 0.044715 * square))
    half = 0.5 * (1.0 + t)
    act = gate * half
    slope = half + 0.5 * gate * (1.0 - t * t) * cubic * (1.0 + 3.0 * 0.044715 * square)
    hidden = (act * upper).astype(bf16)
    grad_hidden = dotf(c, wd, ((1,), (1,)))
    grad_gate = (grad_hidden * upper * slope).astype(bf16)
    grad_upper = (grad_hidden * act).astype(bf16)
    part = dotf(hidden, wd, ((1,), (0,)))
    back = dotf(grad_gate, wg, ((1,), (1,))) + dotf(grad_upper, wu, ((1,), (1,)))
    gd_ref[...] = dotf(hidden, c, ((0,), (0,))).astype(bf16)
    gg_ref[0] = dotf(x, grad_gate, ((0,), (0,))).astype(bf16)
    gu_ref[0] = dotf(x, grad_upper, ((0,), (0,))).astype(bf16)

    @pl.when(pl.program_id(0) == 0)
    def _():
        out_ref[...] = part
        dx_ref[...] = back

    @pl.when(pl.program_id(0) > 0)
    def _():
        out_ref[...] += part
        dx_ref[...] += back


def feed_forward(x, cot, w_gate, w_up, w_down):
    rows, width = x.shape
    blocks, unused, units = w_gate.shape
    whole = pl.BlockSpec((rows, width), lambda i: (0, 0))
    gates = pl.BlockSpec((1, width, units), lambda i: (i, 0, 0))
    downs = pl.BlockSpec((units, width), lambda i: (i, 0))
    return pl.pallas_call(
        ffn_kernel,
        grid=(blocks,),
        in_specs=[whole, whole, gates, gates, downs],
        out_specs=[whole, whole, gates, gates, downs],
        out_shape=[
            jax.ShapeDtypeStruct((rows, width), f32),
            jax.ShapeDtypeStruct((rows, width), f32),
            jax.ShapeDtypeStruct(w_gate.shape, bf16),
            jax.ShapeDtypeStruct(w_up.shape, bf16),
            jax.ShapeDtypeStruct(w_down.shape, bf16),
        ],
        compiler_params=pltpu.CompilerParams(vmem_limit_bytes=56 << 20),
        name="feed_forward",
    )(x, cot, w_gate, w_up, w_down)


def mm(a, b):
    return jnp.dot(a, b, preferred_element_type=f32)


def mm_nt(a, b):
    return dotf(a, b, ((1,), (1,)))


def mm_tn(a, b):
    return dotf(a, b, ((0,), (0,)))


def gather_full(shard, dp_axis, tp_axis):
    part = lax.all_gather(shard, "tp", axis=tp_axis, tiled=True)
    return lax.all_gather(part, "dp", axis=dp_axis, tiled=True)


def scatter_sum(whole, dp_axis, tp_axis):
    part = lax.psum_scatter(whole, "dp", scatter_dimension=dp_axis, tiled=True)
    return lax.psum_scatter(part, "tp", scatter_dimension=tp_axis, tiled=True).astype(f32)


def adam_update(weight, gradient, first_moment, second_moment, factor, decay_now, rate):
    clipped = gradient * factor
    first_new = beta_one * first_moment + (1.0 - beta_one) * clipped
    second_new = beta_two * second_moment + (1.0 - beta_two) * clipped * clipped
    first_hat = first_new / (1.0 - beta_one**STEP)
    second_hat = second_new / (1.0 - beta_two**STEP)
    weight_new = weight - rate * (
        first_hat / (jnp.sqrt(second_hat) + adam_epsilon) + decay_now * weight
    )
    return (first_new, second_new, weight_new)


def per_device(
    rows_in,
    memory,
    lengths,
    mem_lengths,
    cotangent,
    query_w,
    keyval_w,
    out_w,
    cross_query_w,
    cross_keyval_w,
    cross_out_w,
    gateup_w,
    down_w,
    gains,
    rel_table,
    query_m,
    keyval_m,
    out_m,
    cross_query_m,
    cross_keyval_m,
    cross_out_m,
    gateup_m,
    down_m,
    gains_m,
    rel_table_m,
    query_v,
    keyval_v,
    out_v,
    cross_query_v,
    cross_keyval_v,
    cross_out_v,
    gateup_v,
    down_v,
    gains_v,
    rel_table_v,
):
    low = lambda w: w.astype(bf16)
    tp_size = lax.axis_size("tp")
    dp_size = lax.axis_size("dp")
    here = dp_size == 8 and tp_size == 4
    shards = [
        low(query_w),
        low(keyval_w),
        low(out_w),
        low(cross_query_w),
        low(cross_keyval_w),
        low(cross_out_w),
        low(gateup_w[0]),
        low(gateup_w[1]),
        low(down_w),
    ]
    if here:
        specs = [
            Row((), *query_w.shape, tp_size),
            Row((2,), *keyval_w.shape[1:], tp_size),
            Column(out_w.shape[1], out_w.shape[0], tp_size),
            Row((), *cross_query_w.shape, tp_size),
            Row((2,), *cross_keyval_w.shape[1:], tp_size),
            Column(cross_out_w.shape[1], cross_out_w.shape[0], tp_size),
            Block(*gateup_w.shape[1:], tp_size),
            Block(*gateup_w.shape[1:], tp_size),
            Column(down_w.shape[1], down_w.shape[0], tp_size),
        ]
        misc = jnp.concatenate(
            [
                gains,
                jnp.pad(rel_table, ((0, 0), (0, gains.shape[1] - rel_table.shape[1]))),
                jnp.zeros((1, gains.shape[1]), f32),
            ]
        )
        gathered = gather_all(
            [misc] + shards + [rows_in, memory],
            [Block(*misc.shape, tp_size)]
            + specs
            + [Rows(*rows_in.shape, tp_size), Rows(*memory.shape, tp_size)],
            [True] * 10 + [False] * 2,
            tp_size,
        )
        misc_all = gathered[0].reshape(tp_size, dp_size, *misc.shape)
        gain_low = low(misc_all[0, :, :3].transpose(1, 0, 2).reshape(3, -1)).astype(f32)
        table_low = low(
            misc_all[:, :, 3:7, : rel_table.shape[1]].transpose(0, 2, 1, 3)
        ).reshape(rel_table.shape[0] * tp_size, rel_table.shape[1] * dp_size)
        weights = gathered[1:10]
        rows_group, memory_group = gathered[10:]
    else:
        splits = ((0, 1), (1, 2), (1, 0), (0, 1), (1, 2), (1, 0), (1, 0), (1, 0), (1, 0))
        shards[6] = shards[6][None]
        shards[7] = shards[7][None]
        weights = [gather_full(shard, *split) for shard, split in zip(shards, splits)]
        gain_low = lax.all_gather(low(gains), "dp", axis=1, tiled=True).astype(f32)
        table_low = gather_full(low(rel_table), 1, 0)
        rows_group = lax.all_gather(rows_in, "tp", axis=0, tiled=True)
        memory_group = lax.all_gather(memory, "tp", axis=0, tiled=True)
    (
        w_query,
        w_keyval,
        w_out,
        w_cross_query,
        w_cross_keyval,
        w_cross_out,
        w_gate,
        w_up,
        w_down,
    ) = weights

    rows_local = rows_in.shape[0]
    key_rows = rows_group.shape[0]
    buckets = table_low.shape[1]
    own_start = lax.axis_index("tp") * rows_local
    width = key_rows + rows_local
    place_index = jnp.arange(width, dtype=jnp.int32)
    signed = jnp.where(place_index >= key_rows, place_index - width, place_index)
    strip = dotf(
        table_low, bucket_onehot(own_start - signed, buckets).astype(bf16), ((1,), (1,))
    )
    diag_onehot = bucket_onehot(own_start + rows_local - 1 - place_index, buckets)

    residual = rows_in.astype(f32)
    normed_group = norm_rows(rows_group.astype(f32), gain_low[0])
    normed = norm_rows(residual, gain_low[0])
    queries = mm(normed, w_query).astype(bf16)
    keys = mm(normed_group, w_keyval[0]).astype(bf16)
    values = mm(normed_group, w_keyval[1]).astype(bf16)
    self_scalars = jnp.stack([lengths[0], own_start.astype(jnp.int32)])
    context, probs = attn_fwd(queries, keys, values, self_scalars, strip, True)
    middle = residual + mm(context, w_out)

    normed_cross = norm_rows(middle, gain_low[1])
    cross_queries = mm(normed_cross, w_cross_query).astype(bf16)
    memory_keys = mm(memory_group, w_cross_keyval[0]).astype(bf16)
    memory_values = mm(memory_group, w_cross_keyval[1]).astype(bf16)
    cross_scalars = jnp.stack([mem_lengths[0], own_start.astype(jnp.int32)])
    cross_context, cross_probs = attn_fwd(
        cross_queries, memory_keys, memory_values, cross_scalars, None, False
    )
    middle_two = middle + mm(cross_context, w_cross_out)
    normed_three = norm_rows(middle_two, gain_low[2])

    hidden_out, grad_normed_three, grad_gate, grad_up, grad_down = feed_forward(
        normed_three, cotangent, w_gate, w_up, w_down
    )
    block_out = (middle_two + hidden_out).astype(bf16)
    back_three, grad_gain_three = norm_back(grad_normed_three, middle_two, gain_low[2])
    grad_middle_two = cotangent.astype(f32) + back_three

    cross_branch = grad_middle_two.astype(bf16)
    grad_cross_out = mm_tn(cross_context, cross_branch).astype(bf16)
    grad_cross_context = mm_nt(cross_branch, w_cross_out).astype(bf16)
    grad_cross_queries, part_mk, part_mv = attn_bwd(
        cross_queries, memory_keys, memory_values, cross_probs, grad_cross_context, False, width
    )
    grad_memory_kv = lax.psum_scatter(
        jnp.concatenate([part_mk, part_mv], axis=1), "tp", scatter_dimension=0, tiled=True
    )
    kv_wide = part_mk.shape[1]
    grad_cross_query = mm_tn(normed_cross, grad_cross_queries).astype(bf16)
    grad_normed_cross = mm_nt(grad_cross_queries, w_cross_query)
    grad_cross_keyval = jnp.stack(
        [
            mm_tn(memory, grad_memory_kv[:, :kv_wide]).astype(bf16),
            mm_tn(memory, grad_memory_kv[:, kv_wide:]).astype(bf16),
        ]
    )
    grad_memory = mm_nt(grad_memory_kv[:, :kv_wide], w_cross_keyval[0]) + mm_nt(
        grad_memory_kv[:, kv_wide:], w_cross_keyval[1]
    )
    back_cross, grad_gain_cross = norm_back(grad_normed_cross, middle, gain_low[1])
    grad_middle = grad_middle_two + back_cross

    branch = grad_middle.astype(bf16)
    grad_out = mm_tn(context, branch).astype(bf16)
    grad_context = mm_nt(branch, w_out).astype(bf16)
    grad_queries, part_k, part_v, diagonals = attn_bwd(
        queries, keys, values, probs, grad_context, True, width
    )
    grad_keyvals = lax.psum_scatter(
        jnp.concatenate([part_k, part_v], axis=1), "tp", scatter_dimension=0, tiled=True
    )
    grad_table = jnp.dot(
        diagonals.reshape(-1, width), diag_onehot, precision=lax.Precision.HIGHEST
    )
    grad_query = mm_tn(normed, grad_queries).astype(bf16)
    grad_keyval = jnp.stack(
        [
            mm_tn(normed, grad_keyvals[:, :kv_wide]).astype(bf16),
            mm_tn(normed, grad_keyvals[:, kv_wide:]).astype(bf16),
        ]
    )
    grad_normed = (
        mm_nt(grad_queries, w_query)
        + mm_nt(grad_keyvals[:, :kv_wide], w_keyval[0])
        + mm_nt(grad_keyvals[:, kv_wide:], w_keyval[1])
    )
    back_one, grad_gain_one = norm_back(grad_normed, residual, gain_low[0])
    grad_rows = grad_middle + back_one

    gain_terms = jnp.stack([grad_gain_one, grad_gain_cross, grad_gain_three])
    wholes = [
        grad_query,
        grad_keyval,
        grad_out,
        grad_cross_query,
        grad_cross_keyval,
        grad_cross_out,
        grad_gate,
        grad_up,
        grad_down,
    ]
    if here:
        lanes = 128
        small = jnp.concatenate(
            [
                gain_terms.reshape(-1, lanes),
                jnp.pad(grad_table, ((0, 0), (0, lanes - grad_table.shape[1]))),
            ]
        )
        *reduced, small_sum, square_rows = reduce_all(wholes, small, specs, tp_size)
        gains_full = small_sum[: -grad_table.shape[0]].reshape(gain_terms.shape)
        table_full = small_sum[-grad_table.shape[0] :, : grad_table.shape[1]]
        squares_all = jnp.sum(square_rows[:, 0])
    else:
        reduced = [scatter_sum(whole, *split) for whole, split in zip(wholes, splits)]
        reduced[6] = reduced[6][0]
        reduced[7] = reduced[7][0]
        squares = jnp.zeros((), f32)
        for piece in reduced:
            squares = squares + jnp.sum(piece * piece)
        squares_all, gains_full, table_full = lax.psum(
            (squares, gain_terms, grad_table), ("dp", "tp")
        )
    reduced = (*reduced[:6], jnp.stack([reduced[6], reduced[7]]), reduced[8])
    grad_norm = jnp.sqrt(
        squares_all + jnp.sum(gains_full * gains_full) + jnp.sum(table_full * table_full)
    )
    factor = clip_limit / jnp.maximum(grad_norm, clip_limit)
    gains_grad = lax.dynamic_slice_in_dim(
        gains_full, lax.axis_index("dp") * gains.shape[1], gains.shape[1], 1
    )
    table_grad = lax.dynamic_slice(
        table_full,
        (
            lax.axis_index("tp") * rel_table.shape[0],
            lax.axis_index("dp") * rel_table.shape[1],
        ),
        rel_table.shape,
    )
    grad_list = reduced + (gains_grad, table_grad)
    params = (
        query_w,
        keyval_w,
        out_w,
        cross_query_w,
        cross_keyval_w,
        cross_out_w,
        gateup_w,
        down_w,
        gains,
        rel_table,
    )
    firsts = (
        query_m,
        keyval_m,
        out_m,
        cross_query_m,
        cross_keyval_m,
        cross_out_m,
        gateup_m,
        down_m,
        gains_m,
        rel_table_m,
    )
    seconds = (
        query_v,
        keyval_v,
        out_v,
        cross_query_v,
        cross_keyval_v,
        cross_out_v,
        gateup_v,
        down_v,
        gains_v,
        rel_table_v,
    )
    rates = update_rates()
    new_firsts = []
    new_seconds = []
    new_weights = []
    for position in range(10):
        decay_now = decay_rate if position < 8 else 0.0
        first_new, second_new, weight_new = adam_update(
            params[position],
            grad_list[position],
            firsts[position],
            seconds[position],
            factor,
            decay_now,
            rates[position],
        )
        new_firsts.append(first_new)
        new_seconds.append(second_new)
        new_weights.append(weight_new)
    return (
        block_out,
        grad_rows,
        grad_memory,
        grad_norm,
        new_firsts[0],
        new_firsts[1],
        new_firsts[2],
        new_firsts[3],
        new_firsts[4],
        new_firsts[5],
        new_firsts[6],
        new_firsts[7],
        new_firsts[8],
        new_firsts[9],
        new_seconds[0],
        new_seconds[1],
        new_seconds[2],
        new_seconds[3],
        new_seconds[4],
        new_seconds[5],
        new_seconds[6],
        new_seconds[7],
        new_seconds[8],
        new_seconds[9],
        new_weights[0],
        new_weights[1],
        new_weights[2],
        new_weights[3],
        new_weights[4],
        new_weights[5],
        new_weights[6],
        new_weights[7],
        new_weights[8],
        new_weights[9],
    )


def solution(mesh):
    return jax.shard_map(
        per_device,
        mesh=mesh,
        in_specs=(
            P(("dp", "tp"), None),
            P(("dp", "tp"), None),
            P("dp"),
            P("dp"),
            P(("dp", "tp"), None),
            P("dp", "tp"),
            P(None, "dp", "tp"),
            P("tp", "dp"),
            P("dp", "tp"),
            P(None, "dp", "tp"),
            P("tp", "dp"),
            P(None, "dp", "tp"),
            P("tp", "dp"),
            P(None, "dp"),
            P("tp", "dp"),
            P("dp", "tp"),
            P(None, "dp", "tp"),
            P("tp", "dp"),
            P("dp", "tp"),
            P(None, "dp", "tp"),
            P("tp", "dp"),
            P(None, "dp", "tp"),
            P("tp", "dp"),
            P(None, "dp"),
            P("tp", "dp"),
            P("dp", "tp"),
            P(None, "dp", "tp"),
            P("tp", "dp"),
            P("dp", "tp"),
            P(None, "dp", "tp"),
            P("tp", "dp"),
            P(None, "dp", "tp"),
            P("tp", "dp"),
            P(None, "dp"),
            P("tp", "dp"),
        ),
        out_specs=(
            P(("dp", "tp"), None),
            P(("dp", "tp"), None),
            P(("dp", "tp"), None),
            P(),
            P("dp", "tp"),
            P(None, "dp", "tp"),
            P("tp", "dp"),
            P("dp", "tp"),
            P(None, "dp", "tp"),
            P("tp", "dp"),
            P(None, "dp", "tp"),
            P("tp", "dp"),
            P(None, "dp"),
            P("tp", "dp"),
            P("dp", "tp"),
            P(None, "dp", "tp"),
            P("tp", "dp"),
            P("dp", "tp"),
            P(None, "dp", "tp"),
            P("tp", "dp"),
            P(None, "dp", "tp"),
            P("tp", "dp"),
            P(None, "dp"),
            P("tp", "dp"),
            P("dp", "tp"),
            P(None, "dp", "tp"),
            P("tp", "dp"),
            P("dp", "tp"),
            P(None, "dp", "tp"),
            P("tp", "dp"),
            P(None, "dp", "tp"),
            P("tp", "dp"),
            P(None, "dp"),
            P("tp", "dp"),
        ),
        check_vma=False,
    )
```
